32 devices in a mesh: parts: 2 (over x), tensor: 16 (over z, y, core).
Axes of the slice: x: 2, y: 2, z: 4, core: 2. Of those that a mesh axis runs over, the one named last changes fastest.
Arguments:
- layer_input: bfloat16 [2048, 5120], P('parts', 'tensor'), parts along dimension 0, may hold values from -6 to 6
- out_grad: bfloat16 [2048, 5120], P('parts', 'tensor'), parts along dimension 0, may hold values from -6 to 6
- gate_pre: bfloat16 [2048, 27648], P('parts', 'tensor'), parts along dimension 0, may hold values from -6 to 6
- up_pre: bfloat16 [2048, 27648], P('parts', 'tensor'), parts along dimension 0, may hold values from -6 to 6
- down_weight: bfloat16 [27648, 5120], P('tensor'), may hold values from -0.0390625 to 0.0390625
- proj_input: int32 [5120, 64], P('tensor'), may hold values from -1 to 1
- proj_output: int32 [5120, 64], P('tensor'), may hold values from -1 to 1
- proj_hidden: int32 [27648, 64], P('tensor'), may hold values from -1 to 1
- proj_upgrad: int32 [27648, 64], P('tensor'), may hold values from -1 to 1
- queries: bfloat16 [4096, 8192], P('tensor'), may hold values from -0.059814453 to 0.059814453
- example_ids: int32 [2048], P('parts'), parts along dimension 0, may hold values from 0 to 127, never falling along the last dimension, each value on 1 to 16 neighbouring positions
Outputs:
- scores: float32 [256, 4096], P('parts', 'tensor'), parts along dimension 0
The draws below stay inside these ranges and needn't reach their ends.
There are 2 independent parts, one for each index of `parts`. The reference program is written for one: setup_inputs(seed, part) draws one part's arguments, and reference() takes and returns one part's arrays. A program takes and returns all parts, laid end to end along the dimension named above; an argument that names none is the same for every part. Nothing has to cross between parts.
Inputs may be any that keep to these rules, and one draw needn't show every extreme that they name: `proj_input`: values -1, 0 and 1. `proj_output`: values -1, 0 and 1. `proj_hidden`: values -1, 0 and 1. `proj_upgrad`: values -1, 0 and 1. `example_ids`: ids are non-decreasing along the rows; every example 0..127 holds 1 to 16 contiguous rows, and one holds exactly 16.
All inputs are finite; a program needn't handle non-finite values.
Results may differ from the reference program's by a relative error of at most 0.01.
Values may be sent and summed in bfloat16 or wider, within the bound.
A program may use at most 128 MiB of HBM per device.

```python
import math
import jax
import jax.numpy as jnp
import numpy as np
from jax import lax

D = 5120
FF = 27648
RANK = 64
ROWS = 1024
MOST = 16
EXAMPLES = 128
QUERIES = 4096


def place_ends(array, stream_key, smallest, top_value):
    spot = [jax.random.randint(jax.random.fold_in(stream_key, axis), (), 0, length) for axis, length in enumerate(array.shape)]
    widest = array.shape.index(max(array.shape))
    beside = spot[:widest] + [(spot[widest] + 1) % array.shape[widest]] + spot[widest + 1:]
    return array.at[tuple(spot)].set(smallest).at[tuple(beside)].set(top_value)


def level_of(key, dims, pieces, low, high):
    loudness, own = 1.0, jax.random.fold_in(key, 6)
    for axis_at, parts in pieces:
        heights = jnp.exp(jax.random.uniform(jax.random.fold_in(own, axis_at), (parts,), jnp.float32, low / len(pieces), high / len(pieces)))
        loudness = loudness * jnp.repeat(heights, dims[axis_at] // parts).reshape([-1 if axis == axis_at else 1 for axis in range(len(dims))])
    return loudness


def split_up(count, total, limit, slope):
    loads = [(1 << 20) // math.isqrt(rank ** slope) + 1 for rank in range(2, count + 1)]
    rest, counts = total - limit - (count - 1), [1] * (count - 1)
    while rest > 0:
        candidates = [i for i in range(count - 1) if counts[i] < limit]
        pool, left = sum([loads[i] for i in candidates]), rest
        for i in candidates:
            more = min(limit - counts[i], max(1, left * loads[i] // pool), rest)
            counts[i] = counts[i] + more
            rest = rest - more
    return np.array([limit] + counts)


def uneven(own_key, amount, total, reach, slope):
    if amount == 2:
        one = jax.random.randint(own_key, (), max(1, total - reach), min(reach, total - 1) + 1)
        return jnp.stack([one, total - one])
    lengths = jnp.asarray(split_up(amount, total, reach, slope), jnp.int32)
    twos = (amount - 1) // 2
    source_of, receiver = lengths[1:1 + 2 * twos:2], lengths[2:2 + 2 * twos:2]
    slack = jnp.minimum(source_of - 1, reach - receiver)
    passed = jax.random.randint(jax.random.fold_in(own_key, 1), (twos,), 0, 1 << 20) % (slack + 1)
    lengths = lengths.at[1:1 + 2 * twos:2].set(source_of - passed).at[2:2 + 2 * twos:2].set(receiver + passed)
    return lengths[jax.random.permutation(jax.random.fold_in(own_key, 2), amount)]


def gaussian(rng, dims, deviation, reach, pieces=(), held_as=jnp.bfloat16):
    array = jax.random.normal(rng, dims, jnp.float32) * deviation
    if len(pieces) > 0:
        array = level_of(rng, dims, pieces, -0.22, 0.18) * array
    return jnp.clip(array, min=-reach, max=reach).astype(held_as)


def setup_inputs(seed: int = 0, part: int = 0) -> dict:
    arg_keys = jax.random.split(jax.random.key(seed), 12)
    own_keys = jax.random.split(jax.random.fold_in(arg_keys[11], part), 12)
    layer_input = gaussian(own_keys[0], (ROWS, D), 1.0, 6.0, ((1, 16),))
    out_grad = gaussian(own_keys[1], (ROWS, D), 1.0, 6.0, ((1, 16),))
    gate_pre = gaussian(own_keys[2], (ROWS, FF), 1.0, 6.0, ((1, 16),))
    up_pre = gaussian(own_keys[3], (ROWS, FF), 1.0, 6.0, ((1, 16),))
    down_weight = gaussian(arg_keys[4], (FF, D), FF ** -0.5, 0.0390625, ((0, 16),))
    proj_input = place_ends(jax.random.randint(arg_keys[5], (D, RANK), -1, 2), jax.random.fold_in(arg_keys[5], 1), -1, 1).astype(jnp.int32)
    proj_output = place_ends(jax.random.randint(arg_keys[6], (D, RANK), -1, 2), jax.random.fold_in(arg_keys[6], 1), -1, 1).astype(jnp.int32)
    proj_hidden = place_ends(jax.random.randint(arg_keys[7], (FF, RANK), -1, 2), jax.random.fold_in(arg_keys[7], 1), -1, 1).astype(jnp.int32)
    proj_upgrad = place_ends(jax.random.randint(arg_keys[8], (FF, RANK), -1, 2), jax.random.fold_in(arg_keys[8], 1), -1, 1).astype(jnp.int32)
    queries = gaussian(arg_keys[9], (QUERIES, 2 * RANK * RANK), 0.01, 0.059814453, ((0, 16),))
    example_ids = jnp.searchsorted(jnp.cumsum(uneven(own_keys[10], EXAMPLES, ROWS, MOST, 1)), jnp.arange(ROWS), side="right").astype(jnp.int32)
    return {"layer_input": layer_input, "out_grad": out_grad, "gate_pre": gate_pre, "up_pre": up_pre, "down_weight": down_weight, "proj_input": proj_input, "proj_output": proj_output, "proj_hidden": proj_hidden, "proj_upgrad": proj_upgrad, "queries": queries, "example_ids": example_ids}


def factor_scales(rank):
    return jnp.concatenate([
        jnp.full((rank,), (1.5 / D) ** 0.5, jnp.float32),
        jnp.full((rank,), (1.5 / FF) ** 0.5, jnp.float32),
        jnp.full((rank,), (1.5 / FF) ** 0.5, jnp.float32),
        jnp.full((rank,), (1.5 / D) ** 0.5, jnp.float32)])


def kron_rows(factors):
    rank = factors.shape[1] // 4
    count = factors.shape[0]
    wide = factors.astype(jnp.float32)
    a_input = wide[:, :rank]
    a_hidden = wide[:, rank:2 * rank]
    b_upgrad = wide[:, 2 * rank:3 * rank]
    b_output = wide[:, 3 * rank:]
    up_part = (a_input[:, :, None] * b_upgrad[:, None, :]).reshape(count, rank * rank)
    down_part = (a_hidden[:, :, None] * b_output[:, None, :]).reshape(count, rank * rank)
    return jnp.concatenate([up_part, down_part], 1).astype(jnp.bfloat16)


def reference(layer_input, out_grad, gate_pre, up_pre, down_weight, proj_input, proj_output, proj_hidden, proj_upgrad, queries, example_ids):
    hidden_grad = jnp.dot(out_grad, down_weight.T, preferred_element_type=jnp.float32)
    gate_act = jax.nn.silu(gate_pre.astype(jnp.float32))
    hidden = (gate_act * up_pre.astype(jnp.float32)).astype(jnp.bfloat16)
    up_grad = (hidden_grad * gate_act).astype(jnp.bfloat16)
    partial_value = jnp.concatenate([
        jnp.dot(layer_input, proj_input.astype(jnp.bfloat16), preferred_element_type=jnp.float32),
        jnp.dot(hidden, proj_hidden.astype(jnp.bfloat16), preferred_element_type=jnp.float32),
        jnp.dot(up_grad, proj_upgrad.astype(jnp.bfloat16), preferred_element_type=jnp.float32),
        jnp.dot(out_grad, proj_output.astype(jnp.bfloat16), preferred_element_type=jnp.float32)], 1)
    factors = (partial_value * factor_scales(RANK)).astype(jnp.bfloat16)
    rows_all = kron_rows(factors)
    row_scores = jnp.dot(rows_all, queries.T, preferred_element_type=jnp.float32)
    onehot = (example_ids[None, :] == jnp.arange(EXAMPLES, dtype=jnp.int32)[:, None]).astype(jnp.float32)
    return jnp.dot(onehot, row_scores, precision=lax.Precision.HIGHEST)
```

```python
import functools

import jax
import jax.numpy as jnp
from jax import lax
from jax.experimental import pallas as pl
from jax.experimental.pallas import tpu as pltpu
from jax.sharding import PartitionSpec as P

EXAMPLES = 128
MESH = pl.DeviceIdType.MESH
PIECES = 3


def factors_kernel(
    n, chunks, scales,
    og_hbm, li_ref, gate_hbm, up_hbm, w_hbm, pin_ref, pout_ref, phid_ref, pupg_ref,
    out_ref,
    og, gate, up, w, phid, pupg, hid, upg, part, gathered, fact,
    local_sem, send_sem, recv_sem, sum_send, sum_recv, fact_send, fact_recv,
):
    depth = og_hbm.shape[0]
    rows = og.shape[1]
    ff = w.shape[0]
    rank = pin_ref.shape[0]
    lines = n // 4
    width = rows // chunks
    groups = n // 16
    share = width // groups
    me = lax.axis_index("tensor")
    z, y, c = me // 4, (me // 2) % 2, me % 2
    f32 = jnp.float32

    def block(zz, yy, cc):
        return (zz * 2 + yy) * 2 + cc

    loads = [
        pltpu.make_async_copy(og_hbm, og.at[pl.ds(pl.multiple_of(me * depth, 16), depth), :], local_sem.at[0]),
        pltpu.make_async_copy(gate_hbm, gate, local_sem.at[1]),
        pltpu.make_async_copy(up_hbm, up, local_sem.at[2]),
        pltpu.make_async_copy(w_hbm, w, local_sem.at[3]),
    ]
    for load in loads:
        load.start()

    barrier = pltpu.get_barrier_semaphore()

    @pl.loop(1, n)
    def _(step):
        pl.semaphore_signal(barrier, inc=1, device_id={"tensor": lax.rem(me + step, n)}, device_id_type=MESH)

    pl.semaphore_wait(barrier, n - 1)

    def lanes(k):
        return pl.ds(pl.multiple_of(k * width, 128), width)

    def copy(blk, k, slot, target):
        where = og.at[pl.ds(pl.multiple_of(blk * depth, 16), depth), lanes(k)]
        return pltpu.make_async_remote_copy(
            src_ref=where, dst_ref=where, send_sem=send_sem.at[slot, k], recv_sem=recv_sem.at[blk, k],
            device_id={"tensor": target}, device_id_type=MESH,
        )

    def to_core(blk, k):
        return copy(blk, k, blk // 2, block(z, y, 1 - c))

    def to_side(blk, k):
        return copy(blk, k, n // 2 + blk // 4, block(z, 1 - y, c))

    def to_next(blk, k):
        return copy(blk, k, n // 2 + lines + blk // 4, block(jnp.minimum(z + 1, lines - 1), y, c))

    def to_last(blk, k):
        return copy(blk, k, n // 2 + 2 * lines + blk // 4, block(jnp.maximum(z - 1, 0), y, c))

    def arrived(blk, k):
        to_core(blk, k).wait_recv()

    loads[0].wait()

    @pl.loop(0, chunks)
    def _(k):
        @pl.when(z < lines - 1)
        def _():
            to_next(me, k).start()

        @pl.when(z > 0)
        def _():
            to_last(me, k).start()

        to_side(me, k).start()
        to_core(me, k).start()

    def from_side(zz, k):
        blk = block(zz, 1 - y, c)
        arrived(blk, k)
        to_core(blk, k).start()

    def stage(d, k):
        if d < lines:
            @pl.when(z >= d)
            def _():
                blk = block(z - d, y, c)
                arrived(blk, k)

                @pl.when(z < lines - 1)
                def _():
                    to_next(blk, k).start()

                to_side(blk, k).start()
                to_core(blk, k).start()

            @pl.when(z + d < lines)
            def _():
                blk = block(z + d, y, c)
                arrived(blk, k)

                @pl.when(z > 0)
                def _():
                    to_last(blk, k).start()

                to_side(blk, k).start()
                to_core(blk, k).start()

        e = d - 1

        @pl.when(z >= e)
        def _():
            from_side(z - e, k)

        if e > 0:
            @pl.when(z + e < lines)
            def _():
                from_side(z + e, k)

    phid[...] = phid_ref[...].astype(f32).astype(jnp.bfloat16)
    pupg[...] = pupg_ref[...].astype(f32).astype(jnp.bfloat16)
    part[pl.ds(0, rank), :] = jnp.dot(
        pin_ref[...].astype(f32).astype(jnp.bfloat16), li_ref[...], preferred_element_type=f32
    ).astype(jnp.bfloat16)
    mine = og[pl.ds(pl.multiple_of(me * depth, 16), depth), :]
    part[pl.ds(3 * rank, rank), :] = jnp.dot(
        pout_ref[...].astype(f32).astype(jnp.bfloat16), mine, preferred_element_type=f32
    ).astype(jnp.bfloat16)
    for load in loads[1:]:
        load.wait()

    tile = ff // PIECES

    def multiply(t, k):
        at = pl.ds(t * tile, tile)
        grad = jnp.dot(w[at, :], og[:, lanes(k)], preferred_element_type=f32)
        pre = gate[at, lanes(k)].astype(f32)
        act = pre / (1.0 + jnp.exp(-pre))
        hid[at, :] = (act * up[at, lanes(k)].astype(f32)).astype(jnp.bfloat16)
        upg[at, :] = (grad * act).astype(jnp.bfloat16)

    def spot(owner, k):
        return (
            pl.ds(pl.multiple_of((owner // groups) * 16, 16), 16),
            pl.ds(pl.multiple_of(k * width + (owner % groups) * share, 128), share),
        )

    def held(k):
        return pl.ds(pl.multiple_of(k * share, 128), share)

    def sum_copy(other, source, k):
        return pltpu.make_async_remote_copy(
            src_ref=part.at[spot(other, k)], dst_ref=gathered.at[source, :, held(k)],
            send_sem=sum_send.at[other, k], recv_sem=sum_recv.at[source, k],
            device_id={"tensor": other}, device_id_type=MESH,
        )

    def fact_copy(other, owner, k):
        return pltpu.make_async_remote_copy(
            src_ref=fact.at[spot(owner, k)], dst_ref=fact.at[spot(owner, k)],
            send_sem=fact_send.at[other, k], recv_sem=fact_recv.at[owner, k],
            device_id={"tensor": other}, device_id_type=MESH,
        )

    def project(k):
        part[pl.ds(rank, rank), lanes(k)] = jnp.dot(
            phid[...], hid[...], preferred_element_type=f32
        ).astype(jnp.bfloat16)
        part[pl.ds(2 * rank, rank), lanes(k)] = jnp.dot(
            pupg[...], upg[...], preferred_element_type=f32
        ).astype(jnp.bfloat16)

        @pl.loop(1, n)
        def _(step):
            sum_copy(lax.rem(me + step, n), me, k).start()

    def add_up(k):
        gathered[pl.ds(me, 1), :, held(k)] = part[spot(me, k)][None]

        @pl.loop(1, n)
        def _(step):
            other = lax.rem(me + step, n)
            sum_copy(other, other, k).wait_recv()

        total = jnp.zeros((16, share), f32)
        for i in range(n):
            total = total + gathered[i, :, held(k)].astype(f32)
        which = (me // groups) * 16 // rank
        scale = jnp.where((which == 0) | (which == 3), scales[0], scales[1]).astype(f32)
        fact[spot(me, k)] = (total * scale).astype(jnp.bfloat16)

        @pl.loop(1, n)
        def _(step):
            fact_copy(lax.rem(me + step, n), me, k).start()

    @pl.loop(0, chunks + 2)
    def _(k):
        computing = (k > 0) & (k <= chunks)
        for d in range(1, lines + 1):
            @pl.when(k < chunks)
            def _(d=d):
                stage(d, k)

            if d <= PIECES:
                @pl.when(computing)
                def _(d=d):
                    multiply(d - 1, k - 1)

            if d == PIECES:
                @pl.when(computing)
                def _():
                    project(k - 1)

        @pl.when(k > 1)
        def _():
            add_up(k - 2)

        @pl.when(k < chunks)
        def _():
            @pl.loop(0, n // 2)
            def _(chip):
                arrived(chip * 2 + 1 - c, k)

    @pl.loop(0, chunks)
    def _(k):
        @pl.loop(1, n)
        def _(step):
            other = lax.rem(me + step, n)
            fact_copy(other, other, k).wait_recv()
            fact_copy(other, me, k).wait_send()
            sum_copy(other, me, k).wait_send()

        @pl.loop(0, n // 2)
        def _(chip):
            to_core(chip * 2 + c, k).wait_send()

        @pl.loop(0, lines)
        def _(zz):
            blk = block(zz, y, c)
            to_side(blk, k).wait_send()

            @pl.when((zz <= z) & (z < lines - 1))
            def _():
                to_next(blk, k).wait_send()

            @pl.when((zz >= z) & (z > 0))
            def _():
                to_last(blk, k).wait_send()

    out_ref[...] = fact[...]


def scores_kernel(fact_ref, queries_ref, ids_ref, out_ref, kron, wide):
    rank = fact_ref.shape[0] // 4
    width = fact_ref.shape[1]
    f32 = jnp.float32
    wide[...] = fact_ref[...].astype(f32)
    for half, (a, b) in enumerate(((0, 2), (1, 3))):
        right = wide[pl.ds(b * rank, rank), :]
        for i in range(rank):
            left = wide[pl.ds(a * rank + i, 1), :]
            kron[pl.ds((half * rank + i) * rank, rank), :] = (left * right).astype(jnp.bfloat16)
    rows = jnp.dot(queries_ref[...], kron[...], preferred_element_type=f32)
    onehot = (
        lax.broadcasted_iota(jnp.int32, (EXAMPLES, width), 0) == ids_ref[...]
    ).astype(f32).astype(jnp.bfloat16)
    total = jnp.zeros(out_ref.shape, f32)
    rest = rows
    for _ in range(3):
        top = rest.astype(jnp.bfloat16)
        total = total + lax.dot_general(onehot, top, (((1,), (1,)), ((), ())), preferred_element_type=f32)
        rest = rest - top.astype(f32)

    @pl.when(pl.program_id(0) == 0)
    def _():
        out_ref[...] = total

    @pl.when(pl.program_id(0) > 0)
    def _():
        out_ref[...] += total


def per_device(
    n, layer_input, out_grad, gate_pre, up_pre, down_weight,
    proj_input, proj_output, proj_hidden, proj_upgrad, queries, example_ids,
):
    rows, depth = out_grad.shape
    ff, d = down_weight.shape
    rank = proj_input.shape[1]
    chunks = 4 if n <= 16 else 2
    width = rows // chunks
    groups = n // 16
    scales = ((1.5 / d) ** 0.5, (1.5 / (ff * n)) ** 0.5)
    bf16 = jnp.bfloat16
    vmem = pl.BlockSpec(memory_space=pltpu.VMEM)
    hbm = pl.BlockSpec(memory_space=pl.ANY)
    sems = pltpu.SemaphoreType.DMA
    fact = pl.pallas_call(
        functools.partial(factors_kernel, n, chunks, scales),
        out_shape=jax.ShapeDtypeStruct((4 * rank, rows), bf16),
        in_specs=[hbm, vmem, hbm, hbm, hbm, vmem, vmem, vmem, vmem],
        out_specs=vmem,
        scratch_shapes=[
            pltpu.VMEM((d, rows), bf16),
            pltpu.VMEM((ff, rows), bf16),
            pltpu.VMEM((ff, rows), bf16),
            pltpu.VMEM((ff, d), bf16),
            pltpu.VMEM((rank, ff), bf16),
            pltpu.VMEM((rank, ff), bf16),
            pltpu.VMEM((ff, width), bf16),
            pltpu.VMEM((ff, width), bf16),
            pltpu.VMEM((4 * rank, rows), bf16),
            pltpu.VMEM((n, 16, rows // groups), bf16),
            pltpu.VMEM((4 * rank, rows), bf16),
            sems((4,)),
            sems((n // 2 + 3 * (n // 4), chunks)),
            sems((n, chunks)),
            sems((n, chunks)),
            sems((n, chunks)),
            sems((n, chunks)),
            sems((n, chunks)),
        ],
        compiler_params=pltpu.CompilerParams(
            collective_id=0, has_side_effects=True, vmem_limit_bytes=56 * 2**20
        ),
        cost_estimate=pl.CostEstimate(
            flops=2 * rows * ff * d, bytes_accessed=2 * ff * d, transcendentals=rows * ff
        ),
    )(
        out_grad.T, layer_input.T, gate_pre.T, up_pre.T, down_weight,
        proj_input.T, proj_output.T, proj_hidden.T, proj_upgrad.T,
    )
    count = queries.shape[0]
    step = rows // 4
    return pl.pallas_call(
        scores_kernel,
        grid=(4,),
        out_shape=jax.ShapeDtypeStruct((EXAMPLES, count), jnp.float32),
        in_specs=[
            pl.BlockSpec((4 * rank, step), lambda i: (0, i)),
            pl.BlockSpec(queries.shape, lambda i: (0, 0)),
            pl.BlockSpec((1, step), lambda i: (0, i)),
        ],
        out_specs=pl.BlockSpec((EXAMPLES, count), lambda i: (0, 0)),
        scratch_shapes=[
            pltpu.VMEM((2 * rank * rank, step), bf16),
            pltpu.VMEM((4 * rank, step), jnp.float32),
        ],
        compiler_params=pltpu.CompilerParams(vmem_limit_bytes=32 * 2**20),
    )(fact, queries, example_ids[None, :])


def solution(mesh):
    split = P("parts", "tensor")
    rows = P("tensor", None)
    placed = (split,) * 4 + (rows,) * 6 + (P("parts"),)
    return jax.shard_map(
        functools.partial(per_device, mesh.shape["tensor"]),
        mesh=mesh, in_specs=placed, out_specs=split, check_vma=False,
    )
```

```python
import functools

import jax
import jax.numpy as jnp
from jax import lax
from jax.experimental import pallas as pl
from jax.experimental.pallas import tpu as pltpu
from jax.sharding import PartitionSpec as P

EXAMPLES = 128
MESH = pl.DeviceIdType.MESH
PIECES = 3


def factors_kernel(
    n, chunks, scales,
    og_hbm, li_ref, gate_hbm, up_hbm, w_hbm, pin_ref, pout_ref, phid_ref, pupg_ref,
    out_ref,
    og, gate, up, w, phid, pupg, hid, upg, part, gathered, fact,
    local_sem, send_sem, recv_sem, sum_send, sum_recv, fact_send, fact_recv,
):
    depth = og_hbm.shape[0]
    rows = og.shape[1]
    ff = w.shape[0]
    rank = pin_ref.shape[0]
    lines = n // 4
    width = rows // chunks
    groups = n // 16
    share = width // groups
    me = lax.axis_index("tensor")
    z, y, c = me // 4, (me // 2) % 2, me % 2
    f32 = jnp.float32

    def block(zz, yy, cc):
        return (zz * 2 + yy) * 2 + cc

    loads = [
        pltpu.make_async_copy(og_hbm, og.at[pl.ds(pl.multiple_of(me * depth, 16), depth), :], local_sem.at[0]),
        pltpu.make_async_copy(gate_hbm, gate, local_sem.at[1]),
        pltpu.make_async_copy(up_hbm, up, local_sem.at[2]),
        pltpu.make_async_copy(w_hbm, w, local_sem.at[3]),
    ]
    for load in loads:
        load.start()

    barrier = pltpu.get_barrier_semaphore()

    @pl.loop(1, n)
    def _(step):
        pl.semaphore_signal(barrier, inc=1, device_id={"tensor": lax.rem(me + step, n)}, device_id_type=MESH)

    pl.semaphore_wait(barrier, n - 1)

    def lanes(k):
        return pl.ds(pl.multiple_of(k * width, 128), width)

    def copy(blk, k, slot, target):
        where = og.at[pl.ds(pl.multiple_of(blk * depth, 16), depth), lanes(k)]
        return pltpu.make_async_remote_copy(
            src_ref=where, dst_ref=where, send_sem=send_sem.at[slot, k], recv_sem=recv_sem.at[blk, k],
            device_id={"tensor": target}, device_id_type=MESH,
        )

    def to_core(blk, k):
        return copy(blk, k, blk // 2, block(z, y, 1 - c))

    def to_side(blk, k):
        return copy(blk, k, n // 2 + blk // 4, block(z, 1 - y, c))

    def to_next(blk, k):
        return copy(blk, k, n // 2 + lines + blk // 4, block(jnp.minimum(z + 1, lines - 1), y, c))

    def to_last(blk, k):
        return copy(blk, k, n // 2 + 2 * lines + blk // 4, block(jnp.maximum(z - 1, 0), y, c))

    def arrived(blk, k):
        to_core(blk, k).wait_recv()

    loads[0].wait()

    @pl.loop(0, chunks)
    def _(k):
        @pl.when(z < lines - 1)
        def _():
            to_next(me, k).start()

        @pl.when(z > 0)
        def _():
            to_last(me, k).start()

        to_side(me, k).start()
        to_core(me, k).start()

    def from_side(zz, k):
        blk = block(zz, 1 - y, c)
        arrived(blk, k)
        to_core(blk, k).start()

    def stage(d, k):
        if d < lines:
            @pl.when(z >= d)
            def _():
                blk = block(z - d, y, c)
                arrived(blk, k)

                @pl.when(z < lines - 1)
                def _():
                    to_next(blk, k).start()

                to_side(blk, k).start()
                to_core(blk, k).start()

            @pl.when(z + d < lines)
            def _():
                blk = block(z + d, y, c)
                arrived(blk, k)

                @pl.when(z > 0)
                def _():
                    to_last(blk, k).start()

                to_side(blk, k).start()
                to_core(blk, k).start()

        e = d - 1

        @pl.when(z >= e)
        def _():
            from_side(z - e, k)

        if e > 0:
            @pl.when(z + e < lines)
            def _():
                from_side(z + e, k)

    phid[...] = phid_ref[...].astype(f32).astype(jnp.bfloat16)
    pupg[...] = pupg_ref[...].astype(f32).astype(jnp.bfloat16)
    part[pl.ds(0, rank), :] = jnp.dot(
        pin_ref[...].astype(f32).astype(jnp.bfloat16), li_ref[...], preferred_element_type=f32
    ).astype(jnp.bfloat16)
    mine = og[pl.ds(pl.multiple_of(me * depth, 16), depth), :]
    part[pl.ds(3 * rank, rank), :] = jnp.dot(
        pout_ref[...].astype(f32).astype(jnp.bfloat16), mine, preferred_element_type=f32
    ).astype(jnp.bfloat16)

    tile = ff // PIECES

    def multiply(t, k):
        at = pl.ds(t * tile, tile)
        grad = jnp.dot(w[at, :], og[:, lanes(k)], preferred_element_type=f32)
        pre = gate[at, lanes(k)].astype(f32)
        act = pre / (1.0 + jnp.exp(-pre))
        hid[at, :] = (act * up[at, lanes(k)].astype(f32)).astype(jnp.bfloat16)
        upg[at, :] = (grad * act).astype(jnp.bfloat16)

    def spot(owner, k):
        return (
            pl.ds(pl.multiple_of((owner // groups) * 16, 16), 16),
            pl.ds(pl.multiple_of(k * width + (owner % groups) * share, 128), share),
        )

    def held(k):
        return pl.ds(pl.multiple_of(k * share, 128), share)

    def sum_copy(other, source, k):
        return pltpu.make_async_remote_copy(
            src_ref=part.at[spot(other, k)], dst_ref=gathered.at[source, :, held(k)],
            send_sem=sum_send.at[other, k], recv_sem=sum_recv.at[source, k],
            device_id={"tensor": other}, device_id_type=MESH,
        )

    def fact_copy(other, owner, k):
        return pltpu.make_async_remote_copy(
            src_ref=fact.at[spot(owner, k)], dst_ref=fact.at[spot(owner, k)],
            send_sem=fact_send.at[other, k], recv_sem=fact_recv.at[owner, k],
            device_id={"tensor": other}, device_id_type=MESH,
        )

    def project(k):
        part[pl.ds(rank, rank), lanes(k)] = jnp.dot(
            phid[...], hid[...], preferred_element_type=f32
        ).astype(jnp.bfloat16)
        part[pl.ds(2 * rank, rank), lanes(k)] = jnp.dot(
            pupg[...], upg[...], preferred_element_type=f32
        ).astype(jnp.bfloat16)

        @pl.loop(1, n)
        def _(step):
            sum_copy(lax.rem(me + step, n), me, k).start()

    def add_up(k):
        gathered[pl.ds(me, 1), :, held(k)] = part[spot(me, k)][None]

        @pl.loop(1, n)
        def _(step):
            other = lax.rem(me + step, n)
            sum_copy(other, other, k).wait_recv()

        total = jnp.zeros((16, share), f32)
        for i in range(n):
            total = total + gathered[i, :, held(k)].astype(f32)
        which = (me // groups) * 16 // rank
        scale = jnp.where((which == 0) | (which == 3), scales[0], scales[1]).astype(f32)
        fact[spot(me, k)] = (total * scale).astype(jnp.bfloat16)

        @pl.loop(1, n)
        def _(step):
            fact_copy(lax.rem(me + step, n), me, k).start()

    @pl.loop(0, chunks + 2)
    def _(k):
        computing = (k > 0) & (k <= chunks)
        for d in range(1, lines + 1):
            @pl.when(k < chunks)
            def _(d=d):
                stage(d, k)

            if d == 1:
                @pl.when(k == 1)
                def _():
                    for load in loads[1:]:
                        load.wait()

                @pl.when(computing)
                def _():
                    @pl.loop(0, n // 2)
                    def _(chip):
                        arrived(chip * 2 + 1 - c, k - 1)

            if d <= PIECES:
                @pl.when(computing)
                def _(d=d):
                    multiply(d - 1, k - 1)

            if d == PIECES:
                @pl.when(computing)
                def _():
                    project(k - 1)

        @pl.when(k > 1)
        def _():
            add_up(k - 2)

    @pl.loop(0, chunks)
    def _(k):
        @pl.loop(1, n)
        def _(step):
            other = lax.rem(me + step, n)
            fact_copy(other, other, k).wait_recv()
            fact_copy(other, me, k).wait_send()
            sum_copy(other, me, k).wait_send()

        @pl.loop(0, n // 2)
        def _(chip):
            to_core(chip * 2 + c, k).wait_send()

        @pl.loop(0, lines)
        def _(zz):
            blk = block(zz, y, c)
            to_side(blk, k).wait_send()

            @pl.when((zz <= z) & (z < lines - 1))
            def _():
                to_next(blk, k).wait_send()

            @pl.when((zz >= z) & (z > 0))
            def _():
                to_last(blk, k).wait_send()

    out_ref[...] = fact[...]


def scores_kernel(fact_ref, queries_ref, ids_ref, out_ref, kron, wide):
    rank = fact_ref.shape[0] // 4
    width = fact_ref.shape[1]
    f32 = jnp.float32
    wide[...] = fact_ref[...].astype(f32)
    for half, (a, b) in enumerate(((0, 2), (1, 3))):
        right = wide[pl.ds(b * rank, rank), :]
        for i in range(rank):
            left = wide[pl.ds(a * rank + i, 1), :]
            kron[pl.ds((half * rank + i) * rank, rank), :] = (left * right).astype(jnp.bfloat16)
    rows = jnp.dot(queries_ref[...], kron[...], preferred_element_type=f32)
    onehot = (
        lax.broadcasted_iota(jnp.int32, (EXAMPLES, width), 0) == ids_ref[...]
    ).astype(f32).astype(jnp.bfloat16)
    total = jnp.zeros(out_ref.shape, f32)
    rest = rows
    for _ in range(3):
        top = rest.astype(jnp.bfloat16)
        total = total + lax.dot_general(onehot, top, (((1,), (1,)), ((), ())), preferred_element_type=f32)
        rest = rest - top.astype(f32)

    @pl.when(pl.program_id(0) == 0)
    def _():
        out_ref[...] = total

    @pl.when(pl.program_id(0) > 0)
    def _():
        out_ref[...] += total


def per_device(
    n, layer_input, out_grad, gate_pre, up_pre, down_weight,
    proj_input, proj_output, proj_hidden, proj_upgrad, queries, example_ids,
):
    rows, depth = out_grad.shape
    ff, d = down_weight.shape
    rank = proj_input.shape[1]
    chunks = 4 if n <= 16 else 2
    width = rows // chunks
    groups = n // 16
    scales = ((1.5 / d) ** 0.5, (1.5 / (ff * n)) ** 0.5)
    bf16 = jnp.bfloat16
    vmem = pl.BlockSpec(memory_space=pltpu.VMEM)
    hbm = pl.BlockSpec(memory_space=pl.ANY)
    sems = pltpu.SemaphoreType.DMA
    fact = pl.pallas_call(
        functools.partial(factors_kernel, n, chunks, scales),
        out_shape=jax.ShapeDtypeStruct((4 * rank, rows), bf16),
        in_specs=[hbm, vmem, hbm, hbm, hbm, vmem, vmem, vmem, vmem],
        out_specs=vmem,
        scratch_shapes=[
            pltpu.VMEM((d, rows), bf16),
            pltpu.VMEM((ff, rows), bf16),
            pltpu.VMEM((ff, rows), bf16),
            pltpu.VMEM((ff, d), bf16),
            pltpu.VMEM((rank, ff), bf16),
            pltpu.VMEM((rank, ff), bf16),
            pltpu.VMEM((ff, width), bf16),
            pltpu.VMEM((ff, width), bf16),
            pltpu.VMEM((4 * rank, rows), bf16),
            pltpu.VMEM((n, 16, rows // groups), bf16),
            pltpu.VMEM((4 * rank, rows), bf16),
            sems((4,)),
            sems((n // 2 + 3 * (n // 4), chunks)),
            sems((n, chunks)),
            sems((n, chunks)),
            sems((n, chunks)),
            sems((n, chunks)),
            sems((n, chunks)),
        ],
        compiler_params=pltpu.CompilerParams(
            collective_id=0, has_side_effects=True, vmem_limit_bytes=56 * 2**20
        ),
        cost_estimate=pl.CostEstimate(
            flops=2 * rows * ff * d, bytes_accessed=2 * ff * d, transcendentals=rows * ff
        ),
    )(
        out_grad.T, layer_input.T, gate_pre.T, up_pre.T, down_weight,
        proj_input.T, proj_output.T, proj_hidden.T, proj_upgrad.T,
    )
    count = queries.shape[0]
    step = rows // 4
    return pl.pallas_call(
        scores_kernel,
        grid=(4,),
        out_shape=jax.ShapeDtypeStruct((EXAMPLES, count), jnp.float32),
        in_specs=[
            pl.BlockSpec((4 * rank, step), lambda i: (0, i)),
            pl.BlockSpec(queries.shape, lambda i: (0, 0)),
            pl.BlockSpec((1, step), lambda i: (0, i)),
        ],
        out_specs=pl.BlockSpec((EXAMPLES, count), lambda i: (0, 0)),
        scratch_shapes=[
            pltpu.VMEM((2 * rank * rank, step), bf16),
            pltpu.VMEM((4 * rank, step), jnp.float32),
        ],
        compiler_params=pltpu.CompilerParams(vmem_limit_bytes=32 * 2**20),
    )(fact, queries, example_ids[None, :])


def solution(mesh):
    split = P("parts", "tensor")
    rows = P("tensor", None)
    placed = (split,) * 4 + (rows,) * 6 + (P("parts"),)
    return jax.shard_map(
        functools.partial(per_device, mesh.shape["tensor"]),
        mesh=mesh, in_specs=placed, out_specs=split, check_vma=False,
    )
```

```python
import functools

import jax
import jax.numpy as jnp
from jax import lax
from jax.experimental import pallas as pl
from jax.experimental.pallas import tpu as pltpu
from jax.sharding import PartitionSpec as P

EXAMPLES = 128
MESH = pl.DeviceIdType.MESH
PIECES = 3


def factors_kernel(
    n, chunks, scales,
    og_hbm, li_ref, gate_hbm, up_hbm, w_hbm, pin_ref, pout_ref, phid_ref, pupg_ref,
    out_ref,
    og, gate, up, w, phid, pupg, hid, upg, part, gathered, fact,
    local_sem, send_sem, recv_sem, sum_send, sum_recv, fact_send, fact_recv,
):
    depth = og_hbm.shape[0]
    rows = og.shape[1]
    ff = w.shape[0]
    rank = pin_ref.shape[0]
    lines = n // 4
    width = rows // chunks
    groups = n // 16
    share = width // groups
    me = lax.axis_index("tensor")
    z, y, c = me // 4, (me // 2) % 2, me % 2
    f32 = jnp.float32

    def block(zz, yy, cc):
        return (zz * 2 + yy) * 2 + cc

    loads = [
        pltpu.make_async_copy(og_hbm, og.at[pl.ds(pl.multiple_of(me * depth, 16), depth), :], local_sem.at[0]),
        pltpu.make_async_copy(gate_hbm, gate, local_sem.at[1]),
        pltpu.make_async_copy(up_hbm, up, local_sem.at[2]),
        pltpu.make_async_copy(w_hbm, w, local_sem.at[3]),
    ]
    for load in loads:
        load.start()

    barrier = pltpu.get_barrier_semaphore()

    @pl.loop(1, n)
    def _(step):
        pl.semaphore_signal(barrier, inc=1, device_id={"tensor": lax.rem(me + step, n)}, device_id_type=MESH)

    pl.semaphore_wait(barrier, n - 1)

    def lanes(k):
        return pl.ds(pl.multiple_of(k * width, 128), width)

    def copy(blk, k, slot, target):
        where = og.at[pl.ds(pl.multiple_of(blk * depth, 16), depth), lanes(k)]
        return pltpu.make_async_remote_copy(
            src_ref=where, dst_ref=where, send_sem=send_sem.at[slot, k], recv_sem=recv_sem.at[blk, k],
            device_id={"tensor": target}, device_id_type=MESH,
        )

    def to_core(blk, k):
        return copy(blk, k, blk // 2, block(z, y, 1 - c))

    def to_side(blk, k):
        return copy(blk, k, n // 2 + blk // 4, block(z, 1 - y, c))

    def to_next(blk, k):
        return copy(blk, k, n // 2 + lines + blk // 4, block(jnp.minimum(z + 1, lines - 1), y, c))

    def to_last(blk, k):
        return copy(blk, k, n // 2 + 2 * lines + blk // 4, block(jnp.maximum(z - 1, 0), y, c))

    def arrived(blk, k):
        to_core(blk, k).wait_recv()

    loads[0].wait()

    def send_own(k):
        @pl.when(z < lines - 1)
        def _():
            to_next(me, k).start()

        @pl.when(z > 0)
        def _():
            to_last(me, k).start()

        to_side(me, k).start()
        to_core(me, k).start()

    send_own(0)

    def from_side(zz, k):
        blk = block(zz, 1 - y, c)
        arrived(blk, k)
        to_core(blk, k).start()

    def stage(d, k):
        if d < lines:
            @pl.when(z >= d)
            def _():
                blk = block(z - d, y, c)
                arrived(blk, k)

                @pl.when(z < lines - 1)
                def _():
                    to_next(blk, k).start()

                to_side(blk, k).start()
                to_core(blk, k).start()

            @pl.when(z + d < lines)
            def _():
                blk = block(z + d, y, c)
                arrived(blk, k)

                @pl.when(z > 0)
                def _():
                    to_last(blk, k).start()

                to_side(blk, k).start()
                to_core(blk, k).start()

        e = d - 1

        @pl.when(z >= e)
        def _():
            from_side(z - e, k)

        if e > 0:
            @pl.when(z + e < lines)
            def _():
                from_side(z + e, k)

    phid[...] = phid_ref[...].astype(f32).astype(jnp.bfloat16)
    pupg[...] = pupg_ref[...].astype(f32).astype(jnp.bfloat16)
    part[pl.ds(0, rank), :] = jnp.dot(
        pin_ref[...].astype(f32).astype(jnp.bfloat16), li_ref[...], preferred_element_type=f32
    ).astype(jnp.bfloat16)
    mine = og[pl.ds(pl.multiple_of(me * depth, 16), depth), :]
    part[pl.ds(3 * rank, rank), :] = jnp.dot(
        pout_ref[...].astype(f32).astype(jnp.bfloat16), mine, preferred_element_type=f32
    ).astype(jnp.bfloat16)

    tile = ff // PIECES

    def multiply(t, k):
        at = pl.ds(t * tile, tile)
        grad = jnp.dot(w[at, :], og[:, lanes(k)], preferred_element_type=f32)
        pre = gate[at, lanes(k)].astype(f32)
        act = pre / (1.0 + jnp.exp(-pre))
        hid[at, :] = (act * up[at, lanes(k)].astype(f32)).astype(jnp.bfloat16)
        upg[at, :] = (grad * act).astype(jnp.bfloat16)

    def spot(owner, k):
        return (
            pl.ds(pl.multiple_of((owner // groups) * 16, 16), 16),
            pl.ds(pl.multiple_of(k * width + (owner % groups) * share, 128), share),
        )

    def held(k):
        return pl.ds(pl.multiple_of(k * share, 128), share)

    def sum_copy(other, source, k):
        return pltpu.make_async_remote_copy(
            src_ref=part.at[spot(other, k)], dst_ref=gathered.at[source, :, held(k)],
            send_sem=sum_send.at[other, k], recv_sem=sum_recv.at[source, k],
            device_id={"tensor": other}, device_id_type=MESH,
        )

    def fact_copy(other, owner, k):
        return pltpu.make_async_remote_copy(
            src_ref=fact.at[spot(owner, k)], dst_ref=fact.at[spot(owner, k)],
            send_sem=fact_send.at[other, k], recv_sem=fact_recv.at[owner, k],
            device_id={"tensor": other}, device_id_type=MESH,
        )

    def project(k):
        part[pl.ds(rank, rank), lanes(k)] = jnp.dot(
            phid[...], hid[...], preferred_element_type=f32
        ).astype(jnp.bfloat16)
        part[pl.ds(2 * rank, rank), lanes(k)] = jnp.dot(
            pupg[...], upg[...], preferred_element_type=f32
        ).astype(jnp.bfloat16)

        @pl.loop(1, n)
        def _(step):
            sum_copy(lax.rem(me + step, n), me, k).start()

    def add_up(k):
        gathered[pl.ds(me, 1), :, held(k)] = part[spot(me, k)][None]

        @pl.loop(1, n)
        def _(step):
            other = lax.rem(me + step, n)
            sum_copy(other, other, k).wait_recv()

        total = jnp.zeros((16, share), f32)
        for i in range(n):
            total = total + gathered[i, :, held(k)].astype(f32)
        which = (me // groups) * 16 // rank
        scale = jnp.where((which == 0) | (which == 3), scales[0], scales[1]).astype(f32)
        fact[spot(me, k)] = (total * scale).astype(jnp.bfloat16)

        @pl.loop(1, n)
        def _(step):
            fact_copy(lax.rem(me + step, n), me, k).start()

    @pl.loop(0, chunks + 2)
    def _(k):
        computing = (k > 0) & (k <= chunks)
        for d in range(1, lines + 1):
            @pl.when(k < chunks)
            def _(d=d):
                stage(d, k)

            if d == 2:
                @pl.when(k + 1 < chunks)
                def _():
                    send_own(k + 1)

            if d == 1:
                @pl.when(k == 1)
                def _():
                    for load in loads[1:]:
                        load.wait()

                @pl.when(computing)
                def _():
                    @pl.loop(0, n // 2)
                    def _(chip):
                        arrived(chip * 2 + 1 - c, k - 1)

            if d <= PIECES:
                @pl.when(computing)
                def _(d=d):
                    multiply(d - 1, k - 1)

            if d == PIECES:
                @pl.when(computing)
                def _():
                    project(k - 1)

        @pl.when(k > 1)
        def _():
            add_up(k - 2)

    @pl.loop(0, chunks)
    def _(k):
        @pl.loop(1, n)
        def _(step):
            other = lax.rem(me + step, n)
            fact_copy(other, other, k).wait_recv()
            fact_copy(other, me, k).wait_send()
            sum_copy(other, me, k).wait_send()

        @pl.loop(0, n // 2)
        def _(chip):
            to_core(chip * 2 + c, k).wait_send()

        @pl.loop(0, lines)
        def _(zz):
            blk = block(zz, y, c)
            to_side(blk, k).wait_send()

            @pl.when((zz <= z) & (z < lines - 1))
            def _():
                to_next(blk, k).wait_send()

            @pl.when((zz >= z) & (z > 0))
            def _():
                to_last(blk, k).wait_send()

    out_ref[...] = fact[...]


def scores_kernel(fact_ref, queries_ref, ids_ref, out_ref, kron, wide):
    rank = fact_ref.shape[0] // 4
    width = fact_ref.shape[1]
    f32 = jnp.float32
    wide[...] = fact_ref[...].astype(f32)
    for half, (a, b) in enumerate(((0, 2), (1, 3))):
        right = wide[pl.ds(b * rank, rank), :]
        for i in range(rank):
            left = wide[pl.ds(a * rank + i, 1), :]
            kron[pl.ds((half * rank + i) * rank, rank), :] = (left * right).astype(jnp.bfloat16)
    rows = jnp.dot(queries_ref[...], kron[...], preferred_element_type=f32)
    onehot = (
        lax.broadcasted_iota(jnp.int32, (EXAMPLES, width), 0) == ids_ref[...]
    ).astype(f32).astype(jnp.bfloat16)
    total = jnp.zeros(out_ref.shape, f32)
    rest = rows
    for _ in range(3):
        top = rest.astype(jnp.bfloat16)
        total = total + lax.dot_general(onehot, top, (((1,), (1,)), ((), ())), preferred_element_type=f32)
        rest = rest - top.astype(f32)

    @pl.when(pl.program_id(0) == 0)
    def _():
        out_ref[...] = total

    @pl.when(pl.program_id(0) > 0)
    def _():
        out_ref[...] += total


def per_device(
    n, layer_input, out_grad, gate_pre, up_pre, down_weight,
    proj_input, proj_output, proj_hidden, proj_upgrad, queries, example_ids,
):
    rows, depth = out_grad.shape
    ff, d = down_weight.shape
    rank = proj_input.shape[1]
    chunks = 4 if n <= 16 else 2
    width = rows // chunks
    groups = n // 16
    scales = ((1.5 / d) ** 0.5, (1.5 / (ff * n)) ** 0.5)
    bf16 = jnp.bfloat16
    vmem = pl.BlockSpec(memory_space=pltpu.VMEM)
    hbm = pl.BlockSpec(memory_space=pl.ANY)
    sems = pltpu.SemaphoreType.DMA
    fact = pl.pallas_call(
        functools.partial(factors_kernel, n, chunks, scales),
        out_shape=jax.ShapeDtypeStruct((4 * rank, rows), bf16),
        in_specs=[hbm, vmem, hbm, hbm, hbm, vmem, vmem, vmem, vmem],
        out_specs=vmem,
        scratch_shapes=[
            pltpu.VMEM((d, rows), bf16),
            pltpu.VMEM((ff, rows), bf16),
            pltpu.VMEM((ff, rows), bf16),
            pltpu.VMEM((ff, d), bf16),
            pltpu.VMEM((rank, ff), bf16),
            pltpu.VMEM((rank, ff), bf16),
            pltpu.VMEM((ff, width), bf16),
            pltpu.VMEM((ff, width), bf16),
            pltpu.VMEM((4 * rank, rows), bf16),
            pltpu.VMEM((n, 16, rows // groups), bf16),
            pltpu.VMEM((4 * rank, rows), bf16),
            sems((4,)),
            sems((n // 2 + 3 * (n // 4), chunks)),
            sems((n, chunks)),
            sems((n, chunks)),
            sems((n, chunks)),
            sems((n, chunks)),
            sems((n, chunks)),
        ],
        compiler_params=pltpu.CompilerParams(
            collective_id=0, has_side_effects=True, vmem_limit_bytes=56 * 2**20
        ),
        cost_estimate=pl.CostEstimate(
            flops=2 * rows * ff * d, bytes_accessed=2 * ff * d, transcendentals=rows * ff
        ),
    )(
        out_grad.T, layer_input.T, gate_pre.T, up_pre.T, down_weight,
        proj_input.T, proj_output.T, proj_hidden.T, proj_upgrad.T,
    )
    count = queries.shape[0]
    step = rows // 4
    return pl.pallas_call(
        scores_kernel,
        grid=(4,),
        out_shape=jax.ShapeDtypeStruct((EXAMPLES, count), jnp.float32),
        in_specs=[
            pl.BlockSpec((4 * rank, step), lambda i: (0, i)),
            pl.BlockSpec(queries.shape, lambda i: (0, 0)),
            pl.BlockSpec((1, step), lambda i: (0, i)),
        ],
        out_specs=pl.BlockSpec((EXAMPLES, count), lambda i: (0, 0)),
        scratch_shapes=[
            pltpu.VMEM((2 * rank * rank, step), bf16),
            pltpu.VMEM((4 * rank, step), jnp.float32),
        ],
        compiler_params=pltpu.CompilerParams(vmem_limit_bytes=32 * 2**20),
    )(fact, queries, example_ids[None, :])


def solution(mesh):
    split = P("parts", "tensor")
    rows = P("tensor", None)
    placed = (split,) * 4 + (rows,) * 6 + (P("parts"),)
    return jax.shard_map(
        functools.partial(per_device, mesh.shape["tensor"]),
        mesh=mesh, in_specs=placed, out_specs=split, check_vma=False,
    )
```

```python
import functools

import jax
import jax.numpy as jnp
from jax import lax
from jax.experimental import pallas as pl
from jax.experimental.pallas import tpu as pltpu
from jax.sharding import PartitionSpec as P

EXAMPLES = 128
MESH = pl.DeviceIdType.MESH
PIECES = 3


def factors_kernel(
    n, chunks, scales,
    og_hbm, li_ref, gate_hbm, up_hbm, w_hbm, pin_ref, pout_ref, phid_ref, pupg_ref,
    queries_hbm, ids_ref, out_ref,
    og, gate, up, w, phid, pupg, hid, upg, part, gathered, fact, queries, kron, wide,
    local_sem, send_sem, recv_sem, sum_send, sum_recv, fact_send, fact_recv,
):
    depth = og_hbm.shape[0]
    rows = og.shape[1]
    ff = w.shape[0]
    rank = pin_ref.shape[0]
    lines = n // 4
    width = rows // chunks
    groups = n // 16
    share = width // groups
    me = lax.axis_index("tensor")
    z, y, c = me // 4, (me // 2) % 2, me % 2
    f32 = jnp.float32

    def block(zz, yy, cc):
        return (zz * 2 + yy) * 2 + cc

    loads = [
        pltpu.make_async_copy(og_hbm, og.at[pl.ds(pl.multiple_of(me * depth, 16), depth), :], local_sem.at[0]),
        pltpu.make_async_copy(gate_hbm, gate, local_sem.at[1]),
        pltpu.make_async_copy(up_hbm, up, local_sem.at[2]),
        pltpu.make_async_copy(w_hbm, w, local_sem.at[3]),
        pltpu.make_async_copy(queries_hbm, queries, local_sem.at[4]),
    ]
    for load in loads:
        load.start()

    barrier = pltpu.get_barrier_semaphore()

    @pl.loop(1, n)
    def _(step):
        pl.semaphore_signal(barrier, inc=1, device_id={"tensor": lax.rem(me + step, n)}, device_id_type=MESH)

    pl.semaphore_wait(barrier, n - 1)

    def lanes(k):
        return pl.ds(pl.multiple_of(k * width, 128), width)

    def copy(blk, k, slot, target):
        where = og.at[pl.ds(pl.multiple_of(blk * depth, 16), depth), lanes(k)]
        return pltpu.make_async_remote_copy(
            src_ref=where, dst_ref=where, send_sem=send_sem.at[slot, k], recv_sem=recv_sem.at[blk, k],
            device_id={"tensor": target}, device_id_type=MESH,
        )

    def to_core(blk, k):
        return copy(blk, k, blk // 2, block(z, y, 1 - c))

    def to_side(blk, k):
        return copy(blk, k, n // 2 + blk // 4, block(z, 1 - y, c))

    def to_next(blk, k):
        return copy(blk, k, n // 2 + lines + blk // 4, block(jnp.minimum(z + 1, lines - 1), y, c))

    def to_last(blk, k):
        return copy(blk, k, n // 2 + 2 * lines + blk // 4, block(jnp.maximum(z - 1, 0), y, c))

    def arrived(blk, k):
        to_core(blk, k).wait_recv()

    loads[0].wait()

    def send_own(k):
        @pl.when(z < lines - 1)
        def _():
            to_next(me, k).start()

        @pl.when(z > 0)
        def _():
            to_last(me, k).start()

        to_side(me, k).start()
        to_core(me, k).start()

    send_own(0)

    def from_side(zz, k):
        blk = block(zz, 1 - y, c)
        arrived(blk, k)
        to_core(blk, k).start()

    def stage(d, k):
        if d < lines:
            @pl.when(z >= d)
            def _():
                blk = block(z - d, y, c)
                arrived(blk, k)

                @pl.when(z < lines - 1)
                def _():
                    to_next(blk, k).start()

                to_side(blk, k).start()
                to_core(blk, k).start()

            @pl.when(z + d < lines)
            def _():
                blk = block(z + d, y, c)
                arrived(blk, k)

                @pl.when(z > 0)
                def _():
                    to_last(blk, k).start()

                to_side(blk, k).start()
                to_core(blk, k).start()

        e = d - 1

        @pl.when(z >= e)
        def _():
            from_side(z - e, k)

        if e > 0:
            @pl.when(z + e < lines)
            def _():
                from_side(z + e, k)

    phid[...] = phid_ref[...].astype(f32).astype(jnp.bfloat16)
    pupg[...] = pupg_ref[...].astype(f32).astype(jnp.bfloat16)
    part[pl.ds(0, rank), :] = jnp.dot(
        pin_ref[...].astype(f32).astype(jnp.bfloat16), li_ref[...], preferred_element_type=f32
    ).astype(jnp.bfloat16)
    mine = og[pl.ds(pl.multiple_of(me * depth, 16), depth), :]
    part[pl.ds(3 * rank, rank), :] = jnp.dot(
        pout_ref[...].astype(f32).astype(jnp.bfloat16), mine, preferred_element_type=f32
    ).astype(jnp.bfloat16)

    tile = ff // PIECES

    def multiply(t, k):
        at = pl.ds(t * tile, tile)
        grad = jnp.dot(w[at, :], og[:, lanes(k)], preferred_element_type=f32)
        pre = gate[at, lanes(k)].astype(f32)
        act = pre / (1.0 + jnp.exp(-pre))
        hid[at, :] = (act * up[at, lanes(k)].astype(f32)).astype(jnp.bfloat16)
        upg[at, :] = (grad * act).astype(jnp.bfloat16)

    def spot(owner, k):
        return (
            pl.ds(pl.multiple_of((owner // groups) * 16, 16), 16),
            pl.ds(pl.multiple_of(k * width + (owner % groups) * share, 128), share),
        )

    def held(k):
        return pl.ds(pl.multiple_of(k * share, 128), share)

    def sum_copy(other, source, k):
        return pltpu.make_async_remote_copy(
            src_ref=part.at[spot(other, k)], dst_ref=gathered.at[source, :, held(k)],
            send_sem=sum_send.at[other, k], recv_sem=sum_recv.at[source, k],
            device_id={"tensor": other}, device_id_type=MESH,
        )

    def fact_copy(other, owner, k):
        return pltpu.make_async_remote_copy(
            src_ref=fact.at[spot(owner, k)], dst_ref=fact.at[spot(owner, k)],
            send_sem=fact_send.at[other, k], recv_sem=fact_recv.at[owner, k],
            device_id={"tensor": other}, device_id_type=MESH,
        )

    def project(k):
        part[pl.ds(rank, rank), lanes(k)] = jnp.dot(
            phid[...], hid[...], preferred_element_type=f32
        ).astype(jnp.bfloat16)
        part[pl.ds(2 * rank, rank), lanes(k)] = jnp.dot(
            pupg[...], upg[...], preferred_element_type=f32
        ).astype(jnp.bfloat16)

        @pl.loop(1, n)
        def _(step):
            sum_copy(lax.rem(me + step, n), me, k).start()

    def add_up(k):
        gathered[pl.ds(me, 1), :, held(k)] = part[spot(me, k)][None]

        @pl.loop(1, n)
        def _(step):
            other = lax.rem(me + step, n)
            sum_copy(other, other, k).wait_recv()

        total = jnp.zeros((16, share), f32)
        for i in range(n):
            total = total + gathered[i, :, held(k)].astype(f32)
        which = (me // groups) * 16 // rank
        scale = jnp.where((which == 0) | (which == 3), scales[0], scales[1]).astype(f32)
        fact[spot(me, k)] = (total * scale).astype(jnp.bfloat16)

        @pl.loop(1, n)
        def _(step):
            fact_copy(lax.rem(me + step, n), me, k).start()

    out_ref[...] = jnp.zeros(out_ref.shape, f32)

    def score(k):
        @pl.loop(1, n)
        def _(step):
            other = lax.rem(me + step, n)
            fact_copy(other, other, k).wait_recv()

        wide[...] = fact[:, lanes(k)].astype(f32)
        for half, (a, b) in enumerate(((0, 2), (1, 3))):
            right = wide[pl.ds(b * rank, rank), :]
            for i in range(rank):
                left = wide[pl.ds(a * rank + i, 1), :]
                kron[pl.ds((half * rank + i) * rank, rank), :] = (left * right).astype(jnp.bfloat16)
        rest = jnp.dot(queries[...], kron[...], preferred_element_type=f32)
        onehot = (
            lax.broadcasted_iota(jnp.int32, (EXAMPLES, width), 0) == ids_ref[:, lanes(k)]
        ).astype(f32).astype(jnp.bfloat16)
        total = jnp.zeros(out_ref.shape, f32)
        for _ in range(3):
            top = rest.astype(jnp.bfloat16)
            total = total + lax.dot_general(
                onehot, top, (((1,), (1,)), ((), ())), preferred_element_type=f32
            )
            rest = rest - top.astype(f32)
        out_ref[...] += total

    @pl.loop(0, chunks + 3)
    def _(k):
        computing = (k > 0) & (k <= chunks)
        for d in range(1, lines + 1):
            @pl.when(k < chunks)
            def _(d=d):
                stage(d, k)

            if d == 2:
                @pl.when(k + 1 < chunks)
                def _():
                    send_own(k + 1)

            if d == 1:
                @pl.when(k == 1)
                def _():
                    for load in loads[1:]:
                        load.wait()

                @pl.when(computing)
                def _():
                    @pl.loop(0, n // 2)
                    def _(chip):
                        arrived(chip * 2 + 1 - c, k - 1)

            if d <= PIECES:
                @pl.when(computing)
                def _(d=d):
                    multiply(d - 1, k - 1)

            if d == PIECES:
                @pl.when(computing)
                def _():
                    project(k - 1)

        @pl.when((k > 1) & (k < chunks + 2))
        def _():
            add_up(k - 2)

        @pl.when(k > 2)
        def _():
            score(k - 3)

    @pl.loop(0, chunks)
    def _(k):
        @pl.loop(1, n)
        def _(step):
            other = lax.rem(me + step, n)
            fact_copy(other, me, k).wait_send()
            sum_copy(other, me, k).wait_send()

        @pl.loop(0, n // 2)
        def _(chip):
            to_core(chip * 2 + c, k).wait_send()

        @pl.loop(0, lines)
        def _(zz):
            blk = block(zz, y, c)
            to_side(blk, k).wait_send()

            @pl.when((zz <= z) & (z < lines - 1))
            def _():
                to_next(blk, k).wait_send()

            @pl.when((zz >= z) & (z > 0))
            def _():
                to_last(blk, k).wait_send()


def per_device(
    n, layer_input, out_grad, gate_pre, up_pre, down_weight,
    proj_input, proj_output, proj_hidden, proj_upgrad, queries, example_ids,
):
    rows, depth = out_grad.shape
    ff, d = down_weight.shape
    rank = proj_input.shape[1]
    chunks = 4 if n <= 16 else 2
    width = rows // chunks
    groups = n // 16
    scales = ((1.5 / d) ** 0.5, (1.5 / (ff * n)) ** 0.5)
    bf16 = jnp.bfloat16
    vmem = pl.BlockSpec(memory_space=pltpu.VMEM)
    hbm = pl.BlockSpec(memory_space=pl.ANY)
    sems = pltpu.SemaphoreType.DMA
    count = queries.shape[0]
    return pl.pallas_call(
        functools.partial(factors_kernel, n, chunks, scales),
        out_shape=jax.ShapeDtypeStruct((EXAMPLES, count), jnp.float32),
        in_specs=[hbm, vmem, hbm, hbm, hbm, vmem, vmem, vmem, vmem, hbm, vmem],
        out_specs=vmem,
        scratch_shapes=[
            pltpu.VMEM((d, rows), bf16),
            pltpu.VMEM((ff, rows), bf16),
            pltpu.VMEM((ff, rows), bf16),
            pltpu.VMEM((ff, d), bf16),
            pltpu.VMEM((rank, ff), bf16),
            pltpu.VMEM((rank, ff), bf16),
            pltpu.VMEM((ff, width), bf16),
            pltpu.VMEM((ff, width), bf16),
            pltpu.VMEM((4 * rank, rows), bf16),
            pltpu.VMEM((n, 16, rows // groups), bf16),
            pltpu.VMEM((4 * rank, rows), bf16),
            pltpu.VMEM(queries.shape, bf16),
            pltpu.VMEM((queries.shape[1], width), bf16),
            pltpu.VMEM((4 * rank, width), jnp.float32),
            sems((5,)),
            sems((n // 2 + 3 * (n // 4), chunks)),
            sems((n, chunks)),
            sems((n, chunks)),
            sems((n, chunks)),
            sems((n, chunks)),
            sems((n, chunks)),
        ],
        compiler_params=pltpu.CompilerParams(
            collective_id=0, has_side_effects=True, vmem_limit_bytes=56 * 2**20
        ),
        cost_estimate=pl.CostEstimate(
            flops=2 * rows * ff * d, bytes_accessed=2 * ff * d, transcendentals=rows * ff
        ),
    )(
        out_grad.T, layer_input.T, gate_pre.T, up_pre.T, down_weight,
        proj_input.T, proj_output.T, proj_hidden.T, proj_upgrad.T,
        queries, example_ids[None, :],
    )


def solution(mesh):
    split = P("parts", "tensor")
    rows = P("tensor", None)
    placed = (split,) * 4 + (rows,) * 6 + (P("parts"),)
    return jax.shard_map(
        functools.partial(per_device, mesh.shape["tensor"]),
        mesh=mesh, in_specs=placed, out_specs=split, check_vma=False,
    )
```

```python
import functools

import jax
import jax.numpy as jnp
from jax import lax
from jax.experimental import pallas as pl
from jax.experimental.pallas import tpu as pltpu
from jax.sharding import PartitionSpec as P

EXAMPLES = 128
MESH = pl.DeviceIdType.MESH
PIECES = 3


def factors_kernel(
    n, chunks, scales,
    og_hbm, li_ref, gate_hbm, up_hbm, w_hbm, pin_ref, pout_ref, phid_ref, pupg_ref,
    queries_hbm, ids_ref, out_ref,
    og, gate, up, w, phid, pupg, hid, upg, part, gathered, fact, queries, kron, wide,
    local_sem, send_sem, recv_sem, sum_send, sum_recv, fact_send, fact_recv,
):
    depth = og_hbm.shape[0]
    rows = og.shape[1]
    ff = w.shape[0]
    rank = pin_ref.shape[0]
    lines = n // 4
    width = rows // chunks
    groups = n // 16
    share = width // groups
    me = lax.axis_index("tensor")
    z, y, c = me // 4, (me // 2) % 2, me % 2
    f32 = jnp.float32

    def block(zz, yy, cc):
        return (zz * 2 + yy) * 2 + cc

    loads = [
        pltpu.make_async_copy(og_hbm, og.at[pl.ds(pl.multiple_of(me * depth, 16), depth), :], local_sem.at[0]),
        pltpu.make_async_copy(gate_hbm, gate, local_sem.at[1]),
        pltpu.make_async_copy(up_hbm, up, local_sem.at[2]),
        pltpu.make_async_copy(w_hbm, w, local_sem.at[3]),
        pltpu.make_async_copy(queries_hbm, queries, local_sem.at[4]),
    ]
    for load in loads:
        load.start()

    barrier = pltpu.get_barrier_semaphore()

    @pl.loop(1, n)
    def _(step):
        pl.semaphore_signal(barrier, inc=1, device_id={"tensor": lax.rem(me + step, n)}, device_id_type=MESH)

    pl.semaphore_wait(barrier, n - 1)

    def lanes(k):
        return pl.ds(pl.multiple_of(k * width, 128), width)

    def copy(blk, k, slot, target):
        where = og.at[pl.ds(pl.multiple_of(blk * depth, 16), depth), lanes(k)]
        return pltpu.make_async_remote_copy(
            src_ref=where, dst_ref=where, send_sem=send_sem.at[slot, k], recv_sem=recv_sem.at[blk, k],
            device_id={"tensor": target}, device_id_type=MESH,
        )

    def to_core(blk, k):
        return copy(blk, k, blk // 2, block(z, y, 1 - c))

    def to_side(blk, k):
        return copy(blk, k, n // 2 + blk // 4, block(z, 1 - y, c))

    def to_next(blk, k):
        return copy(blk, k, n // 2 + lines + blk // 2, block(jnp.minimum(z + 1, lines - 1), y, c))

    def to_last(blk, k):
        return copy(blk, k, n + lines + blk // 2, block(jnp.maximum(z - 1, 0), y, c))

    def arrived(blk, k):
        to_core(blk, k).wait_recv()

    loads[0].wait()

    def send_own(k):
        @pl.when(z < lines - 1)
        def _():
            to_next(me, k).start()

        @pl.when(z > 0)
        def _():
            to_last(me, k).start()

        to_side(me, k).start()
        to_core(me, k).start()

    send_own(0)

    def from_side(zz, k):
        blk = block(zz, 1 - y, c)
        arrived(blk, k)
        to_core(blk, k).start()

    def stage(d, k):
        if d < lines:
            @pl.when(z >= d)
            def _():
                blk = block(z - d, y, c)
                arrived(blk, k)

                @pl.when(z < lines - 1)
                def _():
                    to_next(blk, k).start()

                to_side(blk, k).start()
                to_core(blk, k).start()

            @pl.when(z + d < lines)
            def _():
                blk = block(z + d, y, c)
                arrived(blk, k)

                @pl.when(z > 0)
                def _():
                    to_last(blk, k).start()

                to_side(blk, k).start()
                to_core(blk, k).start()

        e = d - 1

        @pl.when(z >= e)
        def _():
            from_side(z - e, k)

        if e > 0:
            @pl.when(z + e < lines)
            def _():
                from_side(z + e, k)

    def side_first(d, k):
        def on(blk, up, down):
            arrived(blk, k)
            if up:
                @pl.when(z < lines - 1)
                def _():
                    to_next(blk, k).start()
            if down:
                @pl.when(z > 0)
                def _():
                    to_last(blk, k).start()
            to_core(blk, k).start()

        if d == 1:
            on(block(z, 1 - y, c), True, True)
        if d < lines:
            for yy in (y, 1 - y):
                @pl.when(z >= d)
                def _(yy=yy):
                    on(block(z - d, yy, c), True, False)

                @pl.when(z + d < lines)
                def _(yy=yy):
                    on(block(z + d, yy, c), False, True)

    phid[...] = phid_ref[...].astype(f32).astype(jnp.bfloat16)
    pupg[...] = pupg_ref[...].astype(f32).astype(jnp.bfloat16)
    part[pl.ds(0, rank), :] = jnp.dot(
        pin_ref[...].astype(f32).astype(jnp.bfloat16), li_ref[...], preferred_element_type=f32
    ).astype(jnp.bfloat16)
    mine = og[pl.ds(pl.multiple_of(me * depth, 16), depth), :]
    part[pl.ds(3 * rank, rank), :] = jnp.dot(
        pout_ref[...].astype(f32).astype(jnp.bfloat16), mine, preferred_element_type=f32
    ).astype(jnp.bfloat16)

    tile = ff // PIECES

    def multiply(t, k):
        at = pl.ds(t * tile, tile)
        grad = jnp.dot(w[at, :], og[:, lanes(k)], preferred_element_type=f32)
        pre = gate[at, lanes(k)].astype(f32)
        act = pre / (1.0 + jnp.exp(-pre))
        hid[at, :] = (act * up[at, lanes(k)].astype(f32)).astype(jnp.bfloat16)
        upg[at, :] = (grad * act).astype(jnp.bfloat16)

    def spot(owner, k):
        return (
            pl.ds(pl.multiple_of((owner // groups) * 16, 16), 16),
            pl.ds(pl.multiple_of(k * width + (owner % groups) * share, 128), share),
        )

    def held(k):
        return pl.ds(pl.multiple_of(k * share, 128), share)

    def sum_copy(other, source, k):
        return pltpu.make_async_remote_copy(
            src_ref=part.at[spot(other, k)], dst_ref=gathered.at[source, :, held(k)],
            send_sem=sum_send.at[other, k], recv_sem=sum_recv.at[source, k],
            device_id={"tensor": other}, device_id_type=MESH,
        )

    def fact_copy(other, owner, k):
        return pltpu.make_async_remote_copy(
            src_ref=fact.at[spot(owner, k)], dst_ref=fact.at[spot(owner, k)],
            send_sem=fact_send.at[other, k], recv_sem=fact_recv.at[owner, k],
            device_id={"tensor": other}, device_id_type=MESH,
        )

    def project(k):
        part[pl.ds(rank, rank), lanes(k)] = jnp.dot(
            phid[...], hid[...], preferred_element_type=f32
        ).astype(jnp.bfloat16)
        part[pl.ds(2 * rank, rank), lanes(k)] = jnp.dot(
            pupg[...], upg[...], preferred_element_type=f32
        ).astype(jnp.bfloat16)

        @pl.loop(1, n)
        def _(step):
            sum_copy(lax.rem(me + step, n), me, k).start()

    def add_up(k):
        gathered[pl.ds(me, 1), :, held(k)] = part[spot(me, k)][None]

        @pl.loop(1, n)
        def _(step):
            other = lax.rem(me + step, n)
            sum_copy(other, other, k).wait_recv()

        total = jnp.zeros((16, share), f32)
        for i in range(n):
            total = total + gathered[i, :, held(k)].astype(f32)
        which = (me // groups) * 16 // rank
        scale = jnp.where((which == 0) | (which == 3), scales[0], scales[1]).astype(f32)
        fact[spot(me, k)] = (total * scale).astype(jnp.bfloat16)

        @pl.loop(1, n)
        def _(step):
            fact_copy(lax.rem(me + step, n), me, k).start()

    out_ref[...] = jnp.zeros(out_ref.shape, f32)

    def score(k):
        @pl.loop(1, n)
        def _(step):
            other = lax.rem(me + step, n)
            fact_copy(other, other, k).wait_recv()

        wide[...] = fact[:, lanes(k)].astype(f32)
        for half, (a, b) in enumerate(((0, 2), (1, 3))):
            right = wide[pl.ds(b * rank, rank), :]
            for i in range(rank):
                left = wide[pl.ds(a * rank + i, 1), :]
                kron[pl.ds((half * rank + i) * rank, rank), :] = (left * right).astype(jnp.bfloat16)
        rest = jnp.dot(queries[...], kron[...], preferred_element_type=f32)
        onehot = (
            lax.broadcasted_iota(jnp.int32, (EXAMPLES, width), 0) == ids_ref[:, lanes(k)]
        ).astype(f32).astype(jnp.bfloat16)
        total = jnp.zeros(out_ref.shape, f32)
        for _ in range(3):
            top = rest.astype(jnp.bfloat16)
            total = total + lax.dot_general(
                onehot, top, (((1,), (1,)), ((), ())), preferred_element_type=f32
            )
            rest = rest - top.astype(f32)
        out_ref[...] += total

    @pl.loop(0, chunks + 3)
    def _(k):
        computing = (k > 0) & (k <= chunks)
        for d in range(1, lines + 1):
            @pl.when(k == 0)
            def _(d=d):
                side_first(d, k)

            @pl.when((k > 0) & (k < chunks))
            def _(d=d):
                stage(d, k)

            if d == 2:
                @pl.when(k + 1 < chunks)
                def _():
                    send_own(k + 1)

            if d == 1:
                @pl.when(k == 1)
                def _():
                    for load in loads[1:]:
                        load.wait()

                @pl.when(computing)
                def _():
                    @pl.loop(0, n // 2)
                    def _(chip):
                        arrived(chip * 2 + 1 - c, k - 1)

            if d <= PIECES:
                @pl.when(computing)
                def _(d=d):
                    multiply(d - 1, k - 1)

            if d == PIECES:
                @pl.when(computing)
                def _():
                    project(k - 1)

        @pl.when((k > 1) & (k < chunks + 2))
        def _():
            add_up(k - 2)

        @pl.when(k > 2)
        def _():
            score(k - 3)

    @pl.loop(0, chunks)
    def _(k):
        @pl.loop(1, n)
        def _(step):
            other = lax.rem(me + step, n)
            fact_copy(other, me, k).wait_send()
            sum_copy(other, me, k).wait_send()

        @pl.loop(0, n // 2)
        def _(chip):
            to_core(chip * 2 + c, k).wait_send()

        @pl.loop(0, lines)
        def _(zz):
            blk = block(zz, y, c)
            across = block(zz, 1 - y, c)

            @pl.when((k > 0) | (zz == z))
            def _():
                to_side(blk, k).wait_send()

            @pl.when((zz <= z) & (z < lines - 1))
            def _():
                to_next(blk, k).wait_send()

                @pl.when(k == 0)
                def _():
                    to_next(across, k).wait_send()

            @pl.when((zz >= z) & (z > 0))
            def _():
                to_last(blk, k).wait_send()

                @pl.when(k == 0)
                def _():
                    to_last(across, k).wait_send()


def per_device(
    n, layer_input, out_grad, gate_pre, up_pre, down_weight,
    proj_input, proj_output, proj_hidden, proj_upgrad, queries, example_ids,
):
    rows, depth = out_grad.shape
    ff, d = down_weight.shape
    rank = proj_input.shape[1]
    chunks = 4 if n <= 16 else 2
    width = rows // chunks
    groups = n // 16
    scales = ((1.5 / d) ** 0.5, (1.5 / (ff * n)) ** 0.5)
    bf16 = jnp.bfloat16
    vmem = pl.BlockSpec(memory_space=pltpu.VMEM)
    hbm = pl.BlockSpec(memory_space=pl.ANY)
    sems = pltpu.SemaphoreType.DMA
    count = queries.shape[0]
    return pl.pallas_call(
        functools.partial(factors_kernel, n, chunks, scales),
        out_shape=jax.ShapeDtypeStruct((EXAMPLES, count), jnp.float32),
        in_specs=[hbm, vmem, hbm, hbm, hbm, vmem, vmem, vmem, vmem, hbm, vmem],
        out_specs=vmem,
        scratch_shapes=[
            pltpu.VMEM((d, rows), bf16),
            pltpu.VMEM((ff, rows), bf16),
            pltpu.VMEM((ff, rows), bf16),
            pltpu.VMEM((ff, d), bf16),
            pltpu.VMEM((rank, ff), bf16),
            pltpu.VMEM((rank, ff), bf16),
            pltpu.VMEM((ff, width), bf16),
            pltpu.VMEM((ff, width), bf16),
            pltpu.VMEM((4 * rank, rows), bf16),
            pltpu.VMEM((n, 16, rows // groups), bf16),
            pltpu.VMEM((4 * rank, rows), bf16),
            pltpu.VMEM(queries.shape, bf16),
            pltpu.VMEM((queries.shape[1], width), bf16),
            pltpu.VMEM((4 * rank, width), jnp.float32),
            sems((5,)),
            sems((3 * (n // 2) + n // 4, chunks)),
            sems((n, chunks)),
            sems((n, chunks)),
            sems((n, chunks)),
            sems((n, chunks)),
            sems((n, chunks)),
        ],
        compiler_params=pltpu.CompilerParams(
            collective_id=0, has_side_effects=True, vmem_limit_bytes=56 * 2**20
        ),
        cost_estimate=pl.CostEstimate(
            flops=2 * rows * ff * d, bytes_accessed=2 * ff * d, transcendentals=rows * ff
        ),
    )(
        out_grad.T, layer_input.T, gate_pre.T, up_pre.T, down_weight,
        proj_input.T, proj_output.T, proj_hidden.T, proj_upgrad.T,
        queries, example_ids[None, :],
    )


def solution(mesh):
    split = P("parts", "tensor")
    rows = P("tensor", None)
    placed = (split,) * 4 + (rows,) * 6 + (P("parts"),)
    return jax.shard_map(
        functools.partial(per_device, mesh.shape["tensor"]),
        mesh=mesh, in_specs=placed, out_specs=split, check_vma=False,
    )
```
